256 devices in a mesh: row: 32 (over y, z), col: 8 (over x, core).
Axes of the slice: x: 4, y: 4, z: 8, core: 2. Of those that a mesh axis runs over, the one named last changes fastest.
Arguments:
- image_rows: bfloat16 [24576, 1024], P('row', 'col'), may hold values from -16 to 16, as said below
- text_rows: bfloat16 [24576, 1024], P('col', 'row'), may hold values from -16 to 16, as said below
Outputs:
- loss: float32 [], replicated
- picture_derivative: float32 [24576, 1024], P('row', 'col')
- text_grad: float32 [24576, 1024], P('col', 'row')
The draws below stay inside these ranges and needn't reach their ends.
Inputs may be any that keep to these rules, and one draw needn't show every extreme that they name: `image_rows`: image embeddings, of order one per entry. `text_rows`: text embeddings, of order one per entry.
All inputs are finite; a program needn't handle non-finite values.
Results may differ from the reference program's by a relative error of at most 0.0018.
Values may be sent and summed in bfloat16 or wider, within the bound.
A program may use at most 128 MiB of HBM per device.

```python
import math
import jax
import jax.numpy as jnp
from jax import lax

VECTOR_DIMENSION = 1024
ROWS_DEV = 96
BATCH = 24576
N_ROW = 32
N_COL = 8


def common_pieces(key):
    key_base, key_correction = jax.random.split(jax.random.fold_in(key, 11), 2)
    base = jnp.clip(jax.random.normal(key_base, (BATCH, VECTOR_DIMENSION), jnp.float32), -4.0, 4.0)
    corr = jax.random.uniform(key_correction, (BATCH, 1), jnp.float32, 0.05, 0.3)
    return (base, corr)


def draw_image_rows(key, part):
    base, corr = common_pieces(key)
    values = base
    return values.astype(jnp.bfloat16)


def draw_text_rows(key, part):
    base, corr = common_pieces(key)
    key = jax.random.fold_in(key, 2)
    key_noise = jax.random.fold_in(key, 0)
    noise = jnp.clip(jax.random.normal(key_noise, (BATCH, VECTOR_DIMENSION), jnp.float32), -4.0, 4.0)
    mixed = corr * base + jnp.sqrt(1.0 - corr * corr) * noise
    values = mixed
    return values.astype(jnp.bfloat16)


def setup_inputs(seed: int = 0) -> dict:
    key_list = jax.random.split(jax.random.key(seed), 3)
    image_rows = draw_image_rows(jax.random.fold_in(key_list[2], 71), 0)
    text_rows = draw_text_rows(jax.random.fold_in(key_list[2], 71), 0)
    return dict(image_rows=image_rows, text_rows=text_rows)


sharpness_divisor = 0.25

def reference(image_rows, text_rows):
    similarity_gain = 1.0 / (sharpness_divisor * math.sqrt(VECTOR_DIMENSION))
    block_rows = ROWS_DEV * N_COL
    blocks = image_rows.reshape(N_ROW, block_rows, VECTOR_DIMENSION)
    starts = (jnp.arange(N_ROW) * block_rows).astype(jnp.int32)
    col_ids = jnp.arange(BATCH).astype(jnp.int32)

    def scores_of(block, start):
        logits = jnp.dot(block, text_rows.T, preferred_element_type=jnp.float32) * similarity_gain
        row_ids = start + jnp.arange(block_rows).astype(jnp.int32)
        diag_mask = row_ids[:, None] == col_ids[None, :]
        return (logits, diag_mask)

    def first_pass(carry, inputs):
        col_top, col_sum = carry
        block, start = inputs
        logits, diag_mask = scores_of(block, start)
        row_top = lax.optimization_barrier(jnp.max(logits, axis=1))
        row_lse = row_top + jnp.log(lax.optimization_barrier(jnp.sum(jnp.exp(logits - row_top[:, None]), axis=1)))
        positive = lax.optimization_barrier(jnp.sum(jnp.where(diag_mask, logits, 0.0), axis=1))
        new_top = jnp.maximum(col_top, lax.optimization_barrier(jnp.max(logits, axis=0)))
        col_sum = col_sum * jnp.exp(col_top - new_top) + lax.optimization_barrier(jnp.sum(jnp.exp(logits - new_top[None, :]), axis=0))
        return ((new_top, col_sum), (row_lse, positive))
    init = (jnp.full((BATCH,), -jnp.inf, jnp.float32), jnp.zeros((BATCH,), jnp.float32))
    (col_top, col_sum), (row_lse, positive) = lax.scan(first_pass, init, (blocks, starts))
    col_lse = col_top + jnp.log(col_sum)
    row_lse = row_lse.reshape(BATCH)
    positive = positive.reshape(BATCH)
    loss = (jnp.sum(row_lse - positive) + jnp.sum(col_lse - positive)) / (2.0 * BATCH)

    def second_pass(text_acc, inputs):
        block, start, block_lse = inputs
        logits, diag_mask = scores_of(block, start)
        weights = (jnp.exp(logits - block_lse[:, None]) + jnp.exp(logits - col_lse[None, :]) - 2.0 * diag_mask.astype(jnp.float32)).astype(jnp.bfloat16)
        image_part = jnp.dot(weights, text_rows, preferred_element_type=jnp.float32)
        text_acc = text_acc + jnp.dot(weights.T, block, preferred_element_type=jnp.float32)
        return (text_acc, image_part)
    text_sum, image_sum = lax.scan(second_pass, jnp.zeros((BATCH, VECTOR_DIMENSION), jnp.float32), (blocks, starts, row_lse.reshape(N_ROW, block_rows)))
    factor = similarity_gain / (2.0 * BATCH)
    picture_derivative = factor * image_sum.reshape(BATCH, VECTOR_DIMENSION)
    text_grad = factor * text_sum
    return (loss, picture_derivative, text_grad)
```

```python
import math

import jax
import jax.numpy as jnp
from jax import lax
from jax.experimental import pallas as pl
from jax.experimental.pallas import tpu as pltpu
from jax.sharding import PartitionSpec as P

MESH = pl.DeviceIdType.MESH
LOG2E = 1.4426950408889634
SHARPNESS = 0.25
SUM_TYPE = jnp.float32

PARTS = ((0, 896, 512, "P"), (896, 640, 256, "Q"))
OFFSETS_Z = (4, 3, 5, 2, 6, 1, 7, 0)
OFFSETS_X = (2, 1, 3, 0)


def interleave(*streams):
    streams = list(streams)
    while streams:
        for stream in list(streams):
            try:
                next(stream)
            except StopIteration:
                streams.remove(stream)


def kernel(
    img_raw, txt_raw,
    loss_out, img_out, txt_out,
    img, imgt, txt, logits, w, tg, ig,
    row_m, row_s, col_m, col_s, row_st, col_st, row_lse_b, loss_r, loss_c,
    land_py, land_pz, land_qz, land_qy, land_c, land_x1, land_x2, land_xp, fin, land_o,
    send, recv, local,
):
    half = txt_raw.shape[1] // 2
    rows_own, feat_own = img_raw.shape
    rows = 2 * rows_own
    dim = img.shape[1]
    scale2 = LOG2E / (SHARPNESS * math.sqrt(dim))
    batch = rows * 16
    factor = 1.0 / (SHARPNESS * math.sqrt(dim)) / (2.0 * batch)

    row_id, col_id = lax.axis_index("row"), lax.axis_index("col")
    y, z = row_id // 8, row_id % 8
    x, c = col_id // 2, col_id % 2
    t, a = y // 2, y % 2

    def dev(dx=None, dy=None, dz=None, dc=None):
        dx = x if dx is None else dx
        dy = y if dy is None else dy
        dz = z if dz is None else dz
        dc = c if dc is None else dc
        return (dy * 8 + dz, dx * 2 + dc)

    y_mate = 2 * t + 1 - a
    y_part = 3 - y
    core_mate = dev(dc=1 - c)
    mate = dev(dy=y_mate)
    partner = dev(dy=y_part)
    z_next = {1: dev(dz=(z + 1) % 8), -1: dev(dz=(z + 7) % 8)}
    x_next = {1: dev(dx=(x + 1) % 4), -1: dev(dx=(x + 3) % 4)}

    def slot_of(yv, tv):
        h = (yv // 2 + tv) % 2
        return 2 * ((yv + h) % 2) + h

    g_row = (x * 2 + c) * 2 + t
    g_col = a * 8 + z

    def row_peer(k):
        g = (g_row + k) % 16
        tt = g % 2
        return dev(dx=g // 4, dc=(g // 2) % 2, dy=jnp.where(tt == t, y, 3 - y))

    def col_peer(k):
        g = (g_col + k) % 16
        return dev(dy=2 * t + g // 8, dz=g % 8)

    barrier = pltpu.get_barrier_semaphore()

    def greet(k, _):
        pl.semaphore_signal(barrier, inc=1, device_id=row_peer(k), device_id_type=MESH)
        pl.semaphore_signal(barrier, inc=1, device_id=col_peer(k), device_id_type=MESH)
        return 0

    lax.fori_loop(1, 16, greet, 0)
    pl.semaphore_wait(barrier, 30)

    count = [0]
    unsent = []

    def message(src, dst, device, start=True):
        k = count[0]
        count[0] += 1
        copy = pltpu.make_async_remote_copy(
            src_ref=src, dst_ref=dst, send_sem=send.at[k], recv_sem=recv.at[k],
            device_id=device, device_id_type=MESH,
        )
        if start:
            copy.start()
            unsent.append(copy)
        return copy

    def lanes(start, size):
        return pl.ds(pl.multiple_of(start, 128), size)

    def block(b):
        return pl.ds(pl.multiple_of(b * rows_own, rows_own), rows_own)

    def img_piece(xv, b, tv=t):
        return img.at[block(b), lanes(slot_of(xv, tv) * 256 + c * 128, 128)]

    def txt_unit(av, zv, c0, n):
        return txt.at[av, :, zv, :, pl.ds(c0, n)]

    same = t == c
    copy_img = pltpu.make_async_copy(img_raw, img_piece(x, t), local.at[0])
    copy_img.start()
    copy_txt = pltpu.make_async_copy(
        txt_raw.at[:, lanes(c * half, half)], txt.at[a, 0, z], local.at[1]
    )
    swap_own = message(txt_raw.at[:, lanes((1 - c) * half, half)], txt.at[a, 0, z], core_mate, start=False)
    k = count[0]
    count[0] += 2
    swap_far = [
        pltpu.make_async_remote_copy(
            src_ref=txt_raw.at[:, pl.ds(q * half, half)], dst_ref=txt.at[1 - a, 1, z],
            send_sem=send.at[k + q], recv_sem=recv.at[k],
            device_id=dev(dy=y_part, dc=q), device_id_type=MESH,
        )
        for q in range(2)
    ]
    swap_in = pltpu.make_async_remote_copy(
        src_ref=txt.at[a, 1, z], dst_ref=txt.at[a, 1, z], send_sem=send.at[k], recv_sem=recv.at[k],
        device_id=partner, device_id_type=MESH,
    )

    @pl.when(same)
    def _():
        swap_own.start()
        copy_txt.start()

    @pl.when(jnp.logical_not(same))
    def _():
        swap_far[0].start()
        swap_far[1].start()

    def gather_img():
        to_partner = message(img_raw, img_piece(x, t, 1 - t), partner)
        own = {d: message(img_raw, img_piece(x, t), x_next[d]) for d in (1, -1)}
        cores = [message(img_raw, img_piece(x, t), core_mate)]
        yield
        to_partner.wait_recv()
        other = {d: message(img_piece(x, 1 - t), img_piece(x, 1 - t), x_next[d]) for d in (1, -1)}
        cores.append(message(img_piece(x, 1 - t), img_piece(x, 1 - t), core_mate))
        yield
        xv = {1: (x + 3) % 4, -1: (x + 1) % 4}
        own[1].wait_recv()
        piece = img_piece(xv[1], t)
        far = {1: message(piece, piece, x_next[1])}
        cores.append(message(piece, piece, core_mate))
        own[-1].wait_recv()
        piece = img_piece(xv[-1], t)
        cores.append(message(piece, piece, core_mate))
        yield
        other[-1].wait_recv()
        piece = img_piece(xv[-1], 1 - t)
        far[-1] = message(piece, piece, x_next[-1])
        cores.append(message(piece, piece, core_mate))
        other[1].wait_recv()
        piece = img_piece(xv[1], 1 - t)
        cores.append(message(piece, piece, core_mate))
        yield
        xo = (x + 2) % 4
        far[1].wait_recv()
        cores.append(message(img_piece(xo, t), img_piece(xo, t), core_mate))
        yield
        far[-1].wait_recv()
        cores.append(message(img_piece(xo, 1 - t), img_piece(xo, 1 - t), core_mate))
        yield
        for copy in cores:
            copy.wait_recv()

    def gather_p(c0, n, n1):
        whole = lambda zv: txt_unit(a, zv, c0, n)
        halves = {1: (c0, n1), -1: (c0 + n1, n - n1)}
        ring = {d: message(whole(z), whole(z), z_next[d]) for d in (1, -1)}
        to_mate = [message(whole(z), whole(z), mate)]
        yield
        for hop in (1, 2, 3):
            onward = {}
            for d in (1, -1):
                ring[d].wait_recv()
                zv = (z - d * hop) % 8 if d == 1 else (z + hop) % 8
                unit = whole(zv) if hop < 3 else txt_unit(a, zv, *halves[d])
                onward[d] = message(unit, unit, z_next[d])
                to_mate.append(message(whole(zv), whole(zv), mate))
            ring = onward
            yield
        for d in (1, -1):
            ring[d].wait_recv()
        zv = (z + 4) % 8
        to_mate.append(message(whole(zv), whole(zv), mate))
        yield
        for copy in to_mate:
            copy.wait_recv()

    def gather_q(c0, n, n1):
        halves = {1: (c0, n1), -1: (c0 + n1, n - n1)}
        own = txt_unit(a, z, c0, n)
        rings = {(0, d): message(own, own, z_next[d]) for d in (1, -1)}
        to_mate = message(own, own, mate)
        yield
        to_mate.wait_recv()
        other = txt_unit(1 - a, z, c0, n)
        rings.update({(1, d): message(other, other, z_next[d]) for d in (1, -1)})
        yield
        for hop in (1, 2, 3):
            for which in (0, 1):
                for d in (1, -1):
                    rings[which, d].wait_recv()
                    zv = (z + 8 - d * hop) % 8
                    av = a if which == 0 else 1 - a
                    unit = txt_unit(av, zv, *((c0, n) if hop < 3 else halves[d]))
                    rings[which, d] = message(unit, unit, z_next[d])
                yield
        for copy in rings.values():
            copy.wait_recv()

    image_stream = gather_img()
    next(image_stream)

    @pl.when(same)
    def _():
        copy_txt.wait()

    @pl.when(jnp.logical_not(same))
    def _():
        swap_own.wait_recv()

    swap_in.wait_recv()
    copy_img.wait()
    streams = [image_stream]
    for c0, n, n1, kind in PARTS:
        streams.append((gather_p if kind == "P" else gather_q)(c0, n, n1))
    interleave(*streams)

    row_m[...] = jnp.full_like(row_m, -1e30)
    row_s[...] = jnp.zeros_like(row_s)
    col_m[...] = jnp.full_like(col_m, -1e30)
    col_s[...] = jnp.zeros_like(col_s)
    RB, CB = 256, 512

    def transpose_step(i, _):
        r = pl.ds(pl.multiple_of(i * RB, RB), RB)
        for s in range(4):
            imgt[s // 2, s % 2, :, r] = img[r, s * 256:(s + 1) * 256].T
        return 0

    lax.fori_loop(0, rows // RB, transpose_step, 0)

    def logits_step(i, _):
        r = pl.ds(pl.multiple_of((i % (rows // RB)) * RB, RB), RB)
        cc = lanes((i // (rows // RB)) * CB, CB)
        tv = txt[:, :, :, :, cc].reshape(dim, CB)
        v = jnp.dot(img[r, :], tv, preferred_element_type=jnp.float32) * scale2
        logits[r, cc] = v
        parts = [v[:, j * 128:(j + 1) * 128] for j in range(CB // 128)]
        m_old = row_m[r, :]
        m = m_old
        for p in parts:
            m = jnp.maximum(m, p)
        s = row_s[r, :] * jnp.exp2(m_old - m)
        for p in parts:
            s = s + jnp.exp2(p - m)
        row_m[r, :] = m
        row_s[r, :] = s
        v3 = v.reshape(RB // 8, 8, CB)
        m_old = col_m[:, cc]
        m = jnp.maximum(m_old, jnp.max(v3, axis=0))
        col_s[:, cc] = col_s[:, cc] * jnp.exp2(m_old - m) + jnp.sum(jnp.exp2(v3 - m[None]), axis=0)
        col_m[:, cc] = m
        return 0

    lax.fori_loop(0, (rows // RB) * (half // CB), logits_step, 0)

    y_lo = jnp.where(t == 0, y, 3 - y)
    d0 = 8 * y_lo + z - 8 * x - 4 * t - 2 * c
    d1 = 8 * (3 - y_lo) + z - 8 * x - 4 * t - 2 * c
    has0 = jnp.logical_and(d0 >= 0, d0 <= 1)
    has1 = jnp.logical_and(d1 >= 0, d1 <= 1)
    has = jnp.logical_or(has0, has1)
    diag_row = jnp.where(has1, rows_own, 0)
    diag_col = jnp.where(has1, d1, jnp.where(has0, d0, 0)) * rows_own
    eye = lax.broadcasted_iota(jnp.int32, (128, 128), 0) == lax.broadcasted_iota(jnp.int32, (128, 128), 1)

    def put(stats, g, m, s):
        top = jnp.max(m, axis=0, keepdims=True)
        stats[g, 0:1, :] = top
        stats[g, 1:2, :] = jnp.sum(s * jnp.exp2(m - top), axis=0, keepdims=True)

    put(col_st, g_col, col_m[...], col_s[...])
    col_st[g_col, 2:3, :] = jnp.zeros((1, half), jnp.float32)

    @pl.when(has)
    def _():
        def diag_step(i, _):
            r = pl.ds(pl.multiple_of(diag_row + i * 128, 128), 128)
            cc = lanes(diag_col + i * 128, 128)
            col_st[g_col, 2:3, cc] = jnp.sum(jnp.where(eye, logits[r, cc], 0.0), axis=0, keepdims=True)
            return 0
        lax.fori_loop(0, rows_own // 128, diag_step, 0)

    def exchange(buffer, g, peer):
        k = count[0]
        count[0] += 15

        def one(i):
            return pltpu.make_async_remote_copy(
                src_ref=buffer.at[g], dst_ref=buffer.at[g], send_sem=send.at[k + i - 1], recv_sem=recv.at[k],
                device_id=peer(i), device_id_type=MESH,
            )

        def start(i, _):
            one(i).start()
            return 0

        lax.fori_loop(1, 16, start, 0)
        everything = buffer.at[pl.ds(0, 15)]

        def finish_send(i, _):
            one(i).wait_send()
            return 0

        def wait():
            pltpu.make_async_copy(everything, everything, recv.at[k]).wait()
        return wait, lambda: lax.fori_loop(1, 16, finish_send, 0)

    wait_col, sent_col = exchange(col_st, g_col, col_peer)
    put(row_st, g_row, row_m[...].T, row_s[...].T)
    wait_row, sent_row = exchange(row_st, g_row, row_peer)

    def lse_of(stats):
        m = stats[:, 0, :]
        top = jnp.max(m, axis=0, keepdims=True)
        return top + jnp.log2(jnp.sum(stats[:, 1, :] * jnp.exp2(m - top), axis=0, keepdims=True))

    wait_col()
    col_lse = lse_of(col_st)
    col_m[0:1, :] = col_lse
    pos = jnp.sum(col_st[:, 2, :], axis=0, keepdims=True)
    loss_c[g_row] = jnp.full((1, 128), jnp.sum(col_lse - 2.0 * pos), jnp.float32)
    wait_row()
    row_lse = lse_of(row_st)
    loss_r[g_col] = jnp.full((1, 128), jnp.sum(row_lse), jnp.float32)
    row_lse_b[...] = jnp.broadcast_to(row_lse, (128, rows)).T
    wait_lc, sent_lc = exchange(loss_c, g_row, row_peer)
    wait_lr, sent_lr = exchange(loss_r, g_col, col_peer)

    def weights_step(i, _):
        r = pl.ds(pl.multiple_of((i % (rows // RB)) * RB, RB), RB)
        cc = (i // (rows // RB)) * CB
        rl = row_lse_b[r, :]
        for j in range(CB // 128):
            lj = lanes(cc + j * 128, 128)
            v = logits[r, lj]
            w[r, lj] = (jnp.exp2(v - rl) + jnp.exp2(v - col_m[0:1, lj])).astype(jnp.bfloat16)
        return 0

    lax.fori_loop(0, (rows // RB) * (half // CB), weights_step, 0)

    @pl.when(has)
    def _():
        def diag_step(i, _):
            r = pl.ds(pl.multiple_of(diag_row + i * 128, 128), 128)
            cc = lanes(diag_col + i * 128, 128)
            v = logits[r, cc]
            wv = jnp.exp2(v - row_lse_b[r, :]) + jnp.exp2(v - col_m[0:1, cc])
            w[r, cc] = jnp.where(eye, wv - 2.0, wv).astype(jnp.bfloat16)
            return 0
        lax.fori_loop(0, rows_own // 128, diag_step, 0)

    def text_grad(av, c0, n):
        step = 128
        def go(i, _):
            cc = lanes(c0 + i * step, step)
            wv = w[:, cc]
            v = jnp.dot(imgt[av].reshape(dim // 2, rows), wv, preferred_element_type=jnp.float32)
            tg[av, :, :, :, cc] = v.reshape(2, 8, 32, step).astype(SUM_TYPE)
            return 0
        lax.fori_loop(0, n // step, go, 0)

    def up(v):
        return v.astype(jnp.float32)

    def add(dst, at, src):
        dst[at] = (up(dst[at]) + up(src)).astype(dst.dtype)

    def scatter_p(c0, n, n1):
        cc = pl.ds(c0, n)
        halves = {1: (0, n1), -1: (n1, n - n1)}
        from_mate = [
            message(tg.at[1 - a, :, (z + o) % 8, :, cc], land_py.at[j], mate) for j, o in enumerate(OFFSETS_Z)
        ]
        yield
        def add_mate(j):
            from_mate[j].wait_recv()
            add(tg, (a, slice(None), (z + OFFSETS_Z[j]) % 8, slice(None), cc), land_py[j])
        add_mate(0)
        ring = {}
        for d in (1, -1):
            h0, hn = halves[d]
            ring[d] = message(
                tg.at[a, :, (z + 4) % 8, :, pl.ds(c0 + h0, hn)],
                land_pz.at[(1 - d) // 2, 0, :, :, pl.ds(h0, hn)], z_next[d],
            )
        yield
        for s in (2, 3, 4):
            for d in (1, -1):
                o = (8 + d * (5 - s)) % 8
                add_mate(OFFSETS_Z.index(o))
                ring[d].wait_recv()
                h0, hn = halves[d] if s == 2 else (0, n)
                add(tg, (a, slice(None), (z + o) % 8, slice(None), pl.ds(c0 + h0, hn)),
                    land_pz[(1 - d) // 2, s - 2, :, :, h0:h0 + hn])
                ring[d] = message(tg.at[a, :, (z + o) % 8, :, cc], land_pz.at[(1 - d) // 2, s - 1], z_next[d])
                yield
        from_mate[7].wait_recv()
        v = up(tg[a, :, z, :, cc]) + up(land_py[7])
        for d in (1, -1):
            ring[d].wait_recv()
            v = v + up(land_pz[(1 - d) // 2, 3])
        fin[:, :, cc] = v

    def scatter_q(c0, n, n1):
        cc = pl.ds(c0, n)
        halves = {1: (0, n1), -1: (n1, n - n1)}
        ring = {}
        for d in (1, -1):
            h0, hn = halves[d]
            ring[d] = message(
                tg.at[:, :, (z + 4) % 8, :, pl.ds(c0 + h0, hn)],
                land_qz.at[(1 - d) // 2, 0, :, :, :, pl.ds(h0, hn)], z_next[d],
            )
        yield
        for s in (2, 3, 4):
            for d in (1, -1):
                o = (8 + d * (5 - s)) % 8
                ring[d].wait_recv()
                h0, hn = halves[d] if s == 2 else (0, n)
                add(tg, (slice(None), slice(None), (z + o) % 8, slice(None), pl.ds(c0 + h0, hn)),
                    land_qz[(1 - d) // 2, s - 2, :, :, :, h0:h0 + hn])
                ring[d] = message(tg.at[:, :, (z + o) % 8, :, cc], land_qz.at[(1 - d) // 2, s - 1], z_next[d])
                yield
        for d in (1, -1):
            ring[d].wait_recv()
        v = up(tg[1 - a, :, z, :, cc]) + up(land_qz[0, 3, 1 - a]) + up(land_qz[1, 3, 1 - a])
        tg[1 - a, :, z, :, cc] = v.astype(SUM_TYPE)
        last = message(tg.at[1 - a, :, z, :, cc], land_qy, mate)
        v = up(tg[a, :, z, :, cc]) + up(land_qz[0, 3, a]) + up(land_qz[1, 3, a])
        yield
        last.wait_recv()
        fin[:, :, cc] = v + up(land_qy[...])

    def image_grad(xv):
        s = slot_of(xv, t)
        def go(i, _):
            r = pl.ds(pl.multiple_of(i * RB, RB), RB)
            tv = txt[s // 2, s % 2].reshape(256, half)
            v = lax.dot_general(w[r, :], tv, (((1,), (1,)), ((), ())), preferred_element_type=jnp.float32)
            ig[s, 0, r, :] = v[:, :128].astype(SUM_TYPE)
            ig[s, 1, r, :] = v[:, 128:].astype(SUM_TYPE)
            return 0
        lax.fori_loop(0, rows // RB, go, 0)

    def scatter_img():
        cores = {}
        for o in OFFSETS_X:
            xv = (x + o) % 4
            image_grad(xv)
            cores[o] = message(ig.at[slot_of(xv, t), 1 - c], land_c.at[o], core_mate)
            yield
        def add_core(o):
            cores[o].wait_recv()
            add(ig, (slot_of((x + o) % 4, t), c), land_c[o])
        add_core(2)
        so = slot_of((x + 2) % 4, t)
        first = {}
        for d, b in ((1, t), (-1, 1 - t)):
            first[d] = message(ig.at[so, c, block(b)], land_x1.at[(1 - d) // 2], x_next[d])
        yield
        second = []
        for d, o, b in ((1, 1, t), (-1, 3, 1 - t)):
            s = slot_of((x + o) % 4, t)
            add_core(o)
            second.append(message(
                ig.at[s, c, block(1 - b)], land_x2.at[(1 - d) // 2, block(1 - b)], x_next[d]))
            yield
            first[d].wait_recv()
            add(ig, (s, c, block(b)), land_x1[(1 - d) // 2])
            second.append(message(ig.at[s, c, block(b)], land_x2.at[(1 - d) // 2, block(b)], x_next[d]))
            yield
        cores[0].wait_recv()
        for copy in second:
            copy.wait_recv()
        s = slot_of(x, t)

        def total(b):
            v = up(ig[s, c, block(b)]) + up(land_c[0, block(b)])
            return v + up(land_x2[0, block(b)]) + up(land_x2[1, block(b)])

        land_xp[0] = total(1 - t)
        last = message(land_xp.at[0], land_xp.at[1], partner)
        mine = total(t)
        land_xp[2] = mine
        yield
        last.wait_recv()
        img_out[...] = (land_xp[2] + land_xp[1]) * factor

    (cp, np_, np1, _), (cq, nq, nq1, _) = PARTS
    text_grad(1 - a, cp, np_)
    p_stream = scatter_p(cp, np_, np1)
    next(p_stream)
    text_grad(a, cq, nq)
    text_grad(1 - a, cq, nq)
    q_stream = scatter_q(cq, nq, nq1)
    next(q_stream)
    text_grad(a, cp, np_)
    i_stream = scatter_img()
    interleave(p_stream, q_stream, i_stream)

    k = count[0]
    count[0] += 3
    out_near = pltpu.make_async_remote_copy(
        src_ref=fin.at[0], dst_ref=land_o.at[c], send_sem=send.at[k], recv_sem=recv.at[k],
        device_id=core_mate, device_id_type=MESH,
    )
    in_near = pltpu.make_async_remote_copy(
        src_ref=fin.at[0], dst_ref=land_o.at[1 - c], send_sem=send.at[k], recv_sem=recv.at[k],
        device_id=core_mate, device_id_type=MESH,
    )
    out_far = pltpu.make_async_remote_copy(
        src_ref=fin.at[1], dst_ref=land_o.at[c], send_sem=send.at[k + 1], recv_sem=recv.at[k + 1 + c],
        device_id=dev(dy=y_part, dc=t), device_id_type=MESH,
    )
    in_far = [
        pltpu.make_async_remote_copy(
            src_ref=fin.at[1], dst_ref=land_o.at[q], send_sem=send.at[k + 1], recv_sem=recv.at[k + 1 + q],
            device_id=partner, device_id_type=MESH,
        )
        for q in range(2)
    ]
    out_far.start()

    @pl.when(same)
    def _():
        land_o[c] = fin[0]
        in_near.wait_recv()

    @pl.when(jnp.logical_not(same))
    def _():
        out_near.start()
        in_far[0].wait_recv()
        in_far[1].wait_recv()

    txt_out[:, :half] = land_o[0] * factor
    txt_out[:, half:] = land_o[1] * factor

    wait_lc()
    wait_lr()
    total = jnp.sum(loss_c[...], axis=0) + jnp.sum(loss_r[...], axis=0)
    loss_out[...] = total * (1.0 / (LOG2E * 2.0 * batch))

    out_far.wait_send()

    @pl.when(same)
    def _():
        swap_own.wait_send()

    @pl.when(jnp.logical_not(same))
    def _():
        swap_far[0].wait_send()
        swap_far[1].wait_send()
        out_near.wait_send()

    for copy in unsent:
        copy.wait_send()
    sent_col()
    sent_row()
    sent_lc()
    sent_lr()


def shards(image_rows, text_rows):
    rows_own, feat_own = image_rows.shape
    txt_t = text_rows.T
    cols = txt_t.shape[1]
    half = cols // 2
    rows = 2 * rows_own
    dim = 8 * feat_own
    (_, np_, _, _), (_, nq, _, _) = PARTS
    f32, bf16 = jnp.float32, jnp.bfloat16
    vmem = pltpu.VMEM
    n_sem = 200
    scratch = [
        vmem((rows, dim), bf16),
        vmem((2, 2, 256, rows), bf16),
        vmem((2, 2, 8, 32, half), bf16),
        vmem((rows, half), f32),
        vmem((rows, half), bf16),
        vmem((2, 2, 8, 32, half), SUM_TYPE),
        vmem((4, 2, rows, 128), SUM_TYPE),
        vmem((rows, 128), f32),
        vmem((rows, 128), f32),
        vmem((8, half), f32),
        vmem((8, half), f32),
        vmem((16, 2, rows), f32),
        vmem((16, 3, half), f32),
        vmem((rows, 128), f32),
        vmem((16, 1, 128), f32),
        vmem((16, 1, 128), f32),
        vmem((8, 2, 32, np_), SUM_TYPE),
        vmem((2, 4, 2, 32, np_), SUM_TYPE),
        vmem((2, 4, 2, 2, 32, nq), SUM_TYPE),
        vmem((2, 32, nq), SUM_TYPE),
        vmem((4, rows, 128), SUM_TYPE),
        vmem((2, rows_own, 128), SUM_TYPE),
        vmem((2, rows, 128), SUM_TYPE),
        vmem((3, rows_own, 128), f32),
        vmem((2, 32, half), f32),
        vmem((2, 32, half), f32),
        pltpu.SemaphoreType.DMA((n_sem,)),
        pltpu.SemaphoreType.DMA((n_sem,)),
        pltpu.SemaphoreType.DMA((2,)),
    ]
    loss, img_grad, txt_grad = pl.pallas_call(
        kernel,
        out_shape=(
            jax.ShapeDtypeStruct((1, 128), f32),
            jax.ShapeDtypeStruct((rows_own, feat_own), f32),
            jax.ShapeDtypeStruct((32, cols), f32),
        ),
        in_specs=[pl.BlockSpec(memory_space=pl.ANY)] * 2,
        out_specs=[pl.BlockSpec(memory_space=pltpu.VMEM)] * 3,
        scratch_shapes=scratch,
        compiler_params=pltpu.CompilerParams(
            collective_id=0, has_side_effects=True, vmem_limit_bytes=61 * 1024 * 1024,
        ),
    )(image_rows, txt_t)
    return loss[0, 0], img_grad, txt_grad.T


def solution(mesh):
    return jax.shard_map(
        shards,
        mesh=mesh,
        in_specs=(P("row", "col"), P("col", "row")),
        out_specs=(P(), P("row", "col"), P("col", "row")),
        check_vma=False,
    )
```
